32 devices in a mesh: pipe: 2 (over x), expert: 8 (over z, y), dp: 2 (over core).
Axes of the slice: x: 2, y: 2, z: 4, core: 2. Of those that a mesh axis runs over, the one named last changes fastest.
Arguments:
- saved: bfloat16 [1, 2, 2048, 2560], P(None, 'pipe', ('expert', 'dp')), may hold values from -6 to 6
- cotangent: bfloat16 [2048, 2560], P(('expert', 'dp'), 'pipe'), may hold values from -1.1953125 to 1.1953125
- routes: int32 [1, 2, 2048, 1], P(None, 'pipe', ('expert', 'dp')), may hold values from 0 to 1; in each aligned block of 16 rows (0 to 15, 16 to 31, ..., all dimensions but the last counted through in order) at most 8 rows name the same one
- w_gate: bfloat16 [1, 2, 2048, 2560], P(None, 'pipe', 'expert', 'dp'), may hold values from -0.125 to 0.125
- w_up: bfloat16 [1, 2, 2048, 2560], P(None, 'pipe', 'expert', 'dp'), may hold values from -0.125 to 0.125
- w_down: bfloat16 [1, 2, 2048, 2560], P(None, 'pipe', 'expert', 'dp'), may hold values from -0.0625 to 0.0625
Outputs:
- grad_gate: bfloat16 [1, 2, 2048, 2560], P(None, 'pipe', 'expert', 'dp')
- grad_up: bfloat16 [1, 2, 2048, 2560], P(None, 'pipe', 'expert', 'dp')
The draws below stay inside these ranges and needn't reach their ends.
Inputs may be any that keep to these rules, and one draw needn't show every extreme that they name: In each aligned block of 16 rows of routes (one micro-batch of one device, rows taken in order over all leading dimensions) no expert is named more than 8 times.
All inputs are finite; a program needn't handle non-finite values.
Results may differ from the reference program's by a relative error of at most 0.017.
Values may be sent and summed in bfloat16 or wider, within the bound.
A program may use at most 64 MiB of HBM per device.

```python
import math
import jax
import jax.numpy as jnp
import numpy as np
from jax import lax

D = 2560
HE = 1024
GROUP = 4
V = 1
MICRO = 8
SECTIONS = 2
EXPERTS = 2
HS = 256
HID = 2048
TOK_MB = 16
CAP = 8
TOKENS = 2048
N_DP = 2


def shard_levels(rng, extent, cuts, smallest, high):
    level, own = 1.0, jax.random.fold_in(rng, 6)
    for axis_at, shards_of in cuts:
        heights = jnp.exp(jax.random.uniform(jax.random.fold_in(own, axis_at), (shards_of,), jnp.float32, smallest / len(cuts), high / len(cuts)))
        level = level * jnp.repeat(heights, extent[axis_at] // shards_of).reshape([-1 if axis == axis_at else 1 for axis in range(len(extent))])
    return level


def assign_block(own_key, own, number, rows, count, top, reach, lean):
    sequence = jax.random.permutation(own_key, count)
    packed, ordinary = load_shares(count, rows * top, reach, lean, True), load_shares(count, rows * top, reach, lean, False)
    places = jnp.arange(count)

    def named(sizes, rotation):
        used = int((sizes > 0).sum())
        fixed = max(1, used // 4)
        passed = fixed + (places - fixed + rotation * (used - fixed)) % max(1, count - fixed)
        return jnp.zeros((count,), jnp.int32).at[sequence[jnp.where(places < fixed, places, passed)]].set(jnp.asarray(sizes, jnp.int32))

    sizes = jnp.where(number % 4 == 0, named(packed, number // 4), named(ordinary, number - number // 4 - 1))
    mixed = jax.random.permutation(jax.random.fold_in(own, 3), count)
    giver, sink = mixed[0:count // 2 * 2:2], mixed[1:count // 2 * 2:2]
    margin = jnp.minimum(sizes[giver] - 1, reach - sizes[sink]) // 2
    margin = jnp.where((giver == sequence[0]) | (sink == sequence[0]) | (sizes[sink] == 0), 0, jnp.maximum(margin, 0))
    passed = jax.random.randint(jax.random.fold_in(own, 4), (count // 2,), 0, 1 << 20) % (margin + 1)
    sizes = sizes.at[giver].add(-passed).at[sink].add(passed)
    members = jnp.searchsorted(jnp.cumsum(sizes), jnp.arange(rows * top), side="right").astype(jnp.int32)
    table = members.reshape(top, rows).T
    table = table[jax.random.permutation(jax.random.fold_in(own, 1), rows)]
    rotation = jax.random.randint(jax.random.fold_in(own, 2), (rows, 1), 0, top)
    return jnp.take_along_axis(table, (jnp.arange(top)[None, :] + rotation) % top, axis=1)


def load_shares(count, total, limit, slope, full):
    portions = [(1 << 20) // math.isqrt(grade ** slope) + 1 for grade in range(1, count + 1)]
    largest = limit if full else min(limit, max(-(-total // count), total * portions[0] // sum(portions)))
    least = 1 if total - largest >= count - 1 else 0
    given, spare = [largest] + [least] * (count - 1), total - largest - least * (count - 1)
    while spare > 0:
        movable = [i for i in range(1, count) if given[i] < largest] or [i for i in range(1, count) if given[i] < limit]
        whole, budget = sum([portions[i] for i in movable]), spare
        for i in movable:
            more = min(limit - given[i], max(1, budget * portions[i] // whole), spare)
            given[i] = given[i] + more
            spare = spare - more
    return np.array(given)


def gaussian(own_key, extent, deviation, reach, pieces=(), held_as=jnp.bfloat16):
    gain = shard_levels(own_key, extent, pieces, -0.22, 0.18) if pieces else 1.0
    drawn = jax.random.normal(own_key, extent, jnp.float32) * deviation * gain
    return jnp.minimum(jnp.maximum(drawn, -reach), reach).astype(held_as)


def setup_inputs(seed: int = 0) -> dict:
    keys = jax.random.split(jax.random.key(seed), 7)
    saved = gaussian(keys[0], (V, SECTIONS, TOKENS, D), 1.0, 6.0, ((1, 2), (2, 16)))
    cotangent = gaussian(keys[1], (TOKENS, D), 0.2, 1.1953125, ((0, 16), (1, 2)))
    routes_keys = jax.random.split(jax.random.fold_in(keys[2], 1), V * SECTIONS * TOKENS // TOK_MB)
    routes_turns = jax.random.permutation(jax.random.fold_in(keys[2], 3), V * SECTIONS * TOKENS // TOK_MB)
    routes = jax.vmap(lambda own, number: assign_block(jax.random.fold_in(keys[2], 2), own, number, TOK_MB, EXPERTS, 1, CAP, 0))(routes_keys, routes_turns).reshape((V, SECTIONS, TOKENS, 1))
    w_gate = gaussian(keys[3], (V, SECTIONS, HID, D), D ** -0.5, 0.125, ((1, 2), (2, 8), (3, 2)))
    w_up = gaussian(keys[4], (V, SECTIONS, HID, D), D ** -0.5, 0.125, ((1, 2), (2, 8), (3, 2)))
    w_down = gaussian(keys[5], (V, SECTIONS, HID, D), (8 * HE) ** -0.5, 0.0625, ((1, 2), (2, 8), (3, 2)))
    return {"saved": saved, "cotangent": cotangent, "routes": routes, "w_gate": w_gate, "w_up": w_up, "w_down": w_down}


epsilon = 1e-06

def slot_numbers(route_ids):
    onehot = (route_ids[:, None] == jnp.arange(EXPERTS, dtype=jnp.int32)[None, :]).astype(jnp.int32)
    blocked = onehot.reshape(TOKENS // TOK_MB, TOK_MB, EXPERTS)
    ranking = lax.optimization_barrier(jnp.sum((jnp.cumsum(blocked, axis=1) - blocked) * blocked, axis=2)).reshape(TOKENS)
    block_ids = jnp.arange(TOKENS, dtype=jnp.int32) // TOK_MB
    return (block_ids * CAP + ranking).astype(jnp.int32)

def rounded_sum(total, term):
    kept = lax.optimization_barrier(term.astype(jnp.bfloat16))
    return total + kept.astype(jnp.float32)

def expert_backward(operands):
    unit_rows, grad_rows, gate_w, up_w, down_w = operands
    slot_total = unit_rows.shape[0]
    gate = jnp.dot(unit_rows, gate_w.T, preferred_element_type=jnp.float32)
    up = jnp.dot(unit_rows, up_w.T, preferred_element_type=jnp.float32)
    hidden_grad = jnp.dot(grad_rows, down_w.T, preferred_element_type=jnp.float32)
    sigmoid_gate = jax.nn.sigmoid(gate)
    gate_grad = (hidden_grad * up * sigmoid_gate * (1.0 + gate * (1.0 - sigmoid_gate))).astype(jnp.bfloat16)
    up_grad = (hidden_grad * gate * sigmoid_gate).astype(jnp.bfloat16)
    unit_grad = jnp.zeros((slot_total, D), jnp.float32)
    for slab_index in range(GROUP):
        first = slab_index * HS
        term = jnp.dot(gate_grad[:, first:first + HS], gate_w[first:first + HS], preferred_element_type=jnp.float32)
        term = term + jnp.dot(up_grad[:, first:first + HS], up_w[first:first + HS], preferred_element_type=jnp.float32)
        unit_grad = rounded_sum(unit_grad, term)
    halves = jnp.arange(slot_total, dtype=jnp.int32) // CAP // MICRO % N_DP
    gate_total = jnp.zeros((HE, D), jnp.float32)
    up_total = jnp.zeros((HE, D), jnp.float32)
    for half_index in range(N_DP):
        keep = (halves == half_index)[:, None]
        gate_kept = jnp.where(keep, gate_grad, jnp.zeros_like(gate_grad))
        up_kept = jnp.where(keep, up_grad, jnp.zeros_like(up_grad))
        gate_total = rounded_sum(gate_total, jnp.dot(gate_kept.T, unit_rows, preferred_element_type=jnp.float32))
        up_total = rounded_sum(up_total, jnp.dot(up_kept.T, unit_rows, preferred_element_type=jnp.float32))
    return (unit_grad, gate_total.astype(jnp.bfloat16), up_total.astype(jnp.bfloat16))

def layer_backward(inputs, grad, route_ids, gate_all, up_all, down_all):
    inputs_f = inputs.astype(jnp.float32)
    norm_scale = lax.rsqrt(lax.optimization_barrier(jnp.mean(inputs_f * inputs_f, axis=1, keepdims=True)) + epsilon)
    unit_f = inputs_f * norm_scale
    unit = unit_f.astype(jnp.bfloat16)
    slot_ids = slot_numbers(route_ids)
    slot_total = TOKENS // TOK_MB * CAP
    unit_buffer = jnp.zeros((EXPERTS, slot_total, D), jnp.bfloat16).at[route_ids, slot_ids].set(unit)
    grad_buffer = jnp.zeros((EXPERTS, slot_total, D), jnp.bfloat16).at[route_ids, slot_ids].set(grad)
    unit_grads, gate_grads, up_grads = lax.map(expert_backward, (unit_buffer, grad_buffer, gate_all.reshape(EXPERTS, HE, D), up_all.reshape(EXPERTS, HE, D), down_all.reshape(EXPERTS, HE, D)))
    unit_grad = unit_grads[route_ids, slot_ids]
    norm_grad = norm_scale * (unit_grad - unit_f * lax.optimization_barrier(jnp.mean(unit_grad * unit_f, axis=1, keepdims=True)))
    new_grad = (grad.astype(jnp.float32) + norm_grad).astype(jnp.bfloat16)
    return (new_grad, gate_grads.reshape(HID, D), up_grads.reshape(HID, D))

def reference(saved, cotangent, routes, w_gate, w_up, w_down):
    grad = cotangent
    gate_table = [[None] * SECTIONS for stretch_index in range(V)]
    up_table = [[None] * SECTIONS for stretch_index in range(V)]
    for layer_index in range(V * SECTIONS - 1, -1, -1):
        stretch_index = layer_index // SECTIONS
        section_index = layer_index % SECTIONS
        grad, gate_out, up_out = layer_backward(saved[stretch_index, section_index], grad, routes[stretch_index, section_index, :, 0], w_gate[stretch_index, section_index], w_up[stretch_index, section_index], w_down[stretch_index, section_index])
        gate_table[stretch_index][section_index] = gate_out
        up_table[stretch_index][section_index] = up_out
    grad_gate = jnp.stack([jnp.stack(row_list) for row_list in gate_table])
    grad_up = jnp.stack([jnp.stack(row_list) for row_list in up_table])
    return (grad_gate, grad_up)
```

```python
import functools

import jax
import jax.numpy as jnp
from jax import lax
from jax.experimental import pallas as pl
from jax.experimental.pallas import tpu as pltpu
from jax.sharding import PartitionSpec as P

GROUP = 4
EPSILON = 1e-06
F32 = jnp.float32
BF16 = jnp.bfloat16
MESH = pl.DeviceIdType.MESH


def dot(a, b, a_dim, b_dim):
    return lax.dot_general(a, b, (((a_dim,), (b_dim,)), ((), ())), preferred_element_type=F32)


def kernel(
    sizes,
    saved, cot, routes, wg, wu, wd,
    out_gate, out_up,
    weights, head, place, unit_send, unit_full, grad_in, grad_send, grad_full,
    gate_f, up_f, gate_grad, up_grad, part, part_recv, sums, sums_recv, grad_out,
    out_send, out_recv, out_own,
    w_s, w_r, h_s, h_r, u1_s, u1_r, u2_s, u2_r, g1_s, g1_r, g2_s, g2_r,
    a_s, a_r, b_s, b_r, x_s, x_r, o_s, o_r,
):
    sections, experts, n_dp, chunks, rows, tok, width = sizes
    sec = lax.axis_index("pipe")
    here = lax.axis_index("expert")
    core = lax.axis_index("dp")
    e_me = here // GROUP
    q_me = here % GROUP
    last = sections - 1
    half = width // n_dp

    def copy(src, dst, s_sem, r_sem, where):
        return pltpu.make_async_remote_copy(
            src_ref=src, dst_ref=dst, send_sem=s_sem, recv_sem=r_sem,
            device_id=where, device_id_type=MESH)

    def peer(step):
        e = (e_me + step) % experts
        return e, {"expert": e * GROUP + q_me}

    def member(step):
        q = (q_me + step) % GROUP
        return q, {"expert": e_me * GROUP + q}

    def other(step):
        c = (core + step) % n_dp
        return c, {"dp": c}

    barrier = pltpu.get_barrier_semaphore()
    friends = [peer(i)[1] for i in range(1, experts)] + [member(i)[1] for i in range(1, GROUP)]
    friends += [other(i)[1] for i in range(1, n_dp)]
    friends += [{"pipe": (sec + i) % sections} for i in range(1, sections)]
    for friend in friends:
        pl.semaphore_signal(barrier, inc=1, device_id=friend, device_id_type=MESH)
    pl.semaphore_wait(barrier, len(friends))

    def head_copy():
        return copy(cot, head.at[sec], h_s.at[0], h_r.at[sec], {"pipe": sections - 1 + 0 * sec})

    @pl.when(sec != last)
    def _():
        head_copy().start()

    def scale_of(c):
        x = saved[pl.ds(c * tok, tok), :].astype(F32)
        scale = lax.rsqrt(jnp.mean(x * x, axis=1, keepdims=True) + EPSILON)
        return x * scale, scale

    def spread_one(c, rows_b, send, full, s_sem, r_sem):
        ordered = dot(place[c], rows_b, 0, 0).astype(BF16)
        for e in range(experts):
            send[c, e] = ordered[e * rows:(e + 1) * rows]
        for i in range(1, experts):
            e, where = peer(i)
            copy(send.at[c, e], full.at[c, q_me, e_me], s_sem.at[c, e], r_sem.at[c, e_me], where).start()
        full[c, q_me, e_me] = send[c, e_me]

    def spread_two(c, send, full, s1, r1, s2, r2):
        for i in range(1, experts):
            e, where = peer(i)
            copy(send.at[c, e], full.at[c, q_me, e], s1.at[c, e], r1.at[c, e], where).wait_recv()
        for i in range(1, GROUP):
            q, where = member(i)
            copy(full.at[c, q_me], full.at[c, q_me], s2.at[c, q], r2.at[c, q_me], where).start()

    def spread_end(c, full, s2, r2):
        for i in range(1, GROUP):
            q, where = member(i)
            copy(full.at[c, q_me], full.at[c, q], s2.at[c, q], r2.at[c, q], where).wait_recv()

    for c in range(chunks):
        chosen = routes[pl.ds(c * tok, tok), :]
        lanes = max(128, experts)
        onehot = (chosen == lax.broadcasted_iota(jnp.int32, (tok, lanes), 1)).astype(F32)
        below = (lax.broadcasted_iota(jnp.int32, (tok, tok), 1)
                 < lax.broadcasted_iota(jnp.int32, (tok, tok), 0)).astype(F32)
        ahead = dot(below.astype(BF16), onehot.astype(BF16), 1, 0)
        rank = jnp.sum(ahead * onehot, axis=1, keepdims=True)
        slot = chosen * rows + rank.astype(jnp.int32)
        place[c] = (slot == lax.broadcasted_iota(jnp.int32, (tok, tok), 1)).astype(F32).astype(BF16)
        unit, _ = scale_of(c)
        spread_one(c, unit.astype(BF16), unit_send, unit_full, u1_s, u1_r)

    for k, ref in enumerate((wg, wu, wd)):
        for i in range(1, n_dp):
            d, where = other(i)
            copy(ref, weights.at[k, core], w_s.at[k, d], w_r.at[k, core], where).start()
        weights[k, core] = ref[...]

    @pl.when(sec == last)
    def _():
        cols = width // sections
        for s in range(last):
            copy(cot, head.at[s], h_s.at[0], h_r.at[s], {"pipe": s}).wait_recv()
        for c in range(chunks):
            for s in range(sections):
                source = cot if s == last else head.at[s]
                grad_in[c, :, s * cols:(s + 1) * cols] = source[c * tok:(c + 1) * tok, :]
            spread_one(c, grad_in[c], grad_send, grad_full, g1_s, g1_r)

    for c in range(chunks):
        spread_two(c, unit_send, unit_full, u1_s, u1_r, u2_s, u2_r)

    @pl.when(sec == last)
    def _():
        for c in range(chunks):
            spread_two(c, grad_send, grad_full, g1_s, g1_r, g2_s, g2_r)

    for k, ref in enumerate((wg, wu, wd)):
        for i in range(1, n_dp):
            d, where = other(i)
            copy(ref, weights.at[k, d], w_s.at[k, d], w_r.at[k, d], where).wait_recv()

    per_block = GROUP if GROUP * experts * rows <= 256 else 1
    blocks = [(first, per_block) for first in range(0, GROUP, per_block)]
    block_rows = per_block * experts * rows

    def rows_of(full, c, first, count):
        return full[c, first:first + count].reshape(block_rows, width)

    def project(x, k):
        total = dot(x[:, :half], weights[k, 0], 1, 1)
        for d in range(1, n_dp):
            total = total + dot(x[:, d * half:(d + 1) * half], weights[k, d], 1, 1)
        return total

    for c in range(chunks):
        spread_end(c, unit_full, u2_s, u2_r)
        for first, count in blocks:
            x = rows_of(unit_full, c, first, count)
            at = pl.ds(c * GROUP * experts * rows + first * experts * rows, block_rows)
            gate_f[at, :] = project(x, 0)
            up_f[at, :] = project(x, 1)

    def backward(c):
        spread_end(c, grad_full, g2_s, g2_r)
        for first, count in blocks:
            at = pl.ds(c * GROUP * experts * rows + first * experts * rows, block_rows)
            hidden_grad = project(rows_of(grad_full, c, first, count), 2)
            gate = gate_f[at, :]
            up = up_f[at, :]
            sig = jax.nn.sigmoid(gate)
            gate_g = (hidden_grad * up * sig * (1.0 + gate * (1.0 - sig))).astype(BF16)
            up_g = (hidden_grad * gate * sig).astype(BF16)
            gate_grad[at, :] = gate_g
            up_grad[at, :] = up_g

            @pl.when(sec > 0)
            def _():
                for d in range(n_dp):
                    value = dot(gate_g, weights[0, d], 1, 0) + dot(up_g, weights[1, d], 1, 0)
                    part[c, first:first + count, :, :, d * half:(d + 1) * half] = (
                        value.astype(BF16).reshape(count, experts, rows, half))

        @pl.when(sec > 0)
        def _():
            for i in range(1, GROUP):
                q, where = member(i)
                copy(part.at[c, q], part_recv.at[c, q_me], a_s.at[c, q], a_r.at[c, q_me], where).start()

    def fold(c):
        total = part[c, q_me].astype(F32)
        for i in range(1, GROUP):
            q, where = member(i)
            copy(part.at[c, q], part_recv.at[c, q], a_s.at[c, q], a_r.at[c, q], where).wait_recv()
            total = total + part_recv[c, q].astype(F32)
        sums[c] = total.astype(BF16)
        for i in range(1, experts):
            e, where = peer(i)
            copy(sums.at[c, e], sums_recv.at[c, e_me], b_s.at[c, e], b_r.at[c, e_me], where).start()
        sums_recv[c, e_me] = sums[c, e_me]

    def x_copy(c):
        return copy(grad_out.at[c], grad_in.at[c], x_s.at[c], x_r.at[c],
                    {"pipe": (sec + sections - 1) % sections})

    def finish(c):
        for i in range(1, experts):
            e, where = peer(i)
            copy(sums.at[c, e], sums_recv.at[c, e], b_s.at[c, e], b_r.at[c, e], where).wait_recv()
        unit_g = dot(place[c], sums_recv[c].reshape(tok, width), 1, 0)
        unit, scale = scale_of(c)
        norm = scale * (unit_g - unit * jnp.mean(unit_g * unit, axis=1, keepdims=True))
        grad_out[c] = (grad_in[c].astype(F32) + norm).astype(BF16)
        x_copy(c).start()

    for t in range(chunks + 2):
        if t < chunks:
            @pl.when(sec != last)
            def _():
                x_copy(t).wait_recv()
                spread_one(t, grad_in[t], grad_send, grad_full, g1_s, g1_r)
                spread_two(t, grad_send, grad_full, g1_s, g1_r, g2_s, g2_r)

            backward(t)

        @pl.when(sec > 0)
        def _():
            if 0 <= t - 1 < chunks:
                fold(t - 1)
            if 0 <= t - 2 < chunks:
                finish(t - 2)

    all_rows = chunks * GROUP * experts * rows

    def o_copy(k, i, mine):
        d, where = other(i)
        return copy(out_send.at[k, d], out_recv.at[k, core if mine else d],
                    o_s.at[k, d], o_r.at[k, core if mine else d], where)

    for k, ref in enumerate((gate_grad, up_grad)):
        left = ref[...]
        for d in range(n_dp):
            right = unit_full[:, :, :, :, d * half:(d + 1) * half].reshape(all_rows, half)
            out_send[k, d] = dot(left, right, 0, 0).astype(BF16)
        for i in range(1, n_dp):
            o_copy(k, i, True).start()
    for k, out in enumerate((out_gate, out_up)):
        total = out_send[k, core].astype(F32)
        for i in range(1, n_dp):
            d, _ = other(i)
            o_copy(k, i, False).wait_recv()
            total = total + out_recv[k, d].astype(F32)
        out[...] = total.astype(BF16)

    for k, ref in enumerate((wg, wu, wd)):
        for i in range(1, n_dp):
            d, where = other(i)
            copy(ref, weights.at[k, d], w_s.at[k, d], w_r.at[k, d], where).wait_send()
    for k in range(2):
        for i in range(1, n_dp):
            o_copy(k, i, True).wait_send()

    @pl.when(sec != last)
    def _():
        head_copy().wait_send()

    for c in range(chunks):
        for i in range(1, experts):
            e, where = peer(i)
            copy(unit_send.at[c, e], unit_full.at[c, q_me, e], u1_s.at[c, e], u1_r.at[c, e], where).wait_send()
            copy(grad_send.at[c, e], grad_full.at[c, q_me, e], g1_s.at[c, e], g1_r.at[c, e], where).wait_send()
        for i in range(1, GROUP):
            q, where = member(i)
            copy(unit_full.at[c, q_me], unit_full.at[c, q], u2_s.at[c, q], u2_r.at[c, q], where).wait_send()
            copy(grad_full.at[c, q_me], grad_full.at[c, q], g2_s.at[c, q], g2_r.at[c, q], where).wait_send()

    @pl.when(sec > 0)
    def _():
        for c in range(chunks):
            for i in range(1, GROUP):
                q, where = member(i)
                copy(part.at[c, q], part_recv.at[c, q], a_s.at[c, q], a_r.at[c, q], where).wait_send()
            for i in range(1, experts):
                e, where = peer(i)
                copy(sums.at[c, e], sums_recv.at[c, e], b_s.at[c, e], b_r.at[c, e], where).wait_send()
            x_copy(c).wait_send()


def shards(mesh, saved, cotangent, routes, w_gate, w_up, w_down):
    sections, spots, n_dp = mesh.shape["pipe"], mesh.shape["expert"], mesh.shape["dp"]
    experts = spots // GROUP
    tokens, width = saved.shape[2], saved.shape[3]
    hidden, half = w_gate.shape[2], w_gate.shape[3]
    chunks = max(1, min(4, tokens // (experts * 16)))
    tok = tokens // chunks
    rows = tok // experts
    sizes = (sections, experts, n_dp, chunks, rows, tok, width)
    all_rows = chunks * GROUP * experts * rows
    full = (chunks, GROUP, experts, rows, width)
    own = (chunks, experts, rows, width)
    dma = pltpu.SemaphoreType.DMA
    vm = pltpu.VMEM
    result = jax.ShapeDtypeStruct((hidden, half), BF16)
    scratch = [
        vm((3, n_dp, hidden, half), BF16),
        vm((sections,) + cotangent.shape, BF16),
        vm((chunks, tok, tok), BF16),
        vm(own, BF16), vm(full, BF16),
        vm((chunks, tok, width), BF16),
        vm(own, BF16), vm(full, BF16),
        vm((all_rows, hidden), F32), vm((all_rows, hidden), F32),
        vm((all_rows, hidden), BF16), vm((all_rows, hidden), BF16),
        vm(full, BF16), vm(full, BF16),
        vm(own, BF16), vm(own, BF16),
        vm((chunks, tok, width), BF16),
        vm((2, n_dp, hidden, half), BF16), vm((2, n_dp, hidden, half), BF16),
        vm((8, 128), F32),
        dma((3, n_dp)), dma((3, n_dp)),
        dma((1,)), dma((sections,)),
        dma((chunks, experts)), dma((chunks, experts)),
        dma((chunks, GROUP)), dma((chunks, GROUP)),
        dma((chunks, experts)), dma((chunks, experts)),
        dma((chunks, GROUP)), dma((chunks, GROUP)),
        dma((chunks, GROUP)), dma((chunks, GROUP)),
        dma((chunks, experts)), dma((chunks, experts)),
        dma((chunks,)), dma((chunks,)),
        dma((2, n_dp)), dma((2, n_dp)),
    ]
    flops = 14 * all_rows * hidden * width
    gate, up = pl.pallas_call(
        functools.partial(kernel, sizes),
        out_shape=(result, result),
        in_specs=[pl.BlockSpec(memory_space=pltpu.VMEM)] * 6,
        out_specs=[pl.BlockSpec(memory_space=pltpu.VMEM)] * 2,
        scratch_shapes=scratch,
        compiler_params=pltpu.CompilerParams(
            collective_id=0, has_side_effects=True, vmem_limit_bytes=52 * 1024 * 1024),
        cost_estimate=pl.CostEstimate(
            flops=flops, bytes_accessed=12 * hidden * half, transcendentals=all_rows * hidden),
    )(saved[0, 0], cotangent, routes[0, 0], w_gate[0, 0], w_up[0, 0], w_down[0, 0])
    return gate[None, None], up[None, None]


def solution(mesh):
    weight = P(None, "pipe", "expert", "dp")
    rows = P(None, "pipe", ("expert", "dp"), None)
    in_specs = (rows, P(("expert", "dp"), "pipe"), rows, weight, weight, weight)
    return jax.shard_map(
        functools.partial(shards, mesh), mesh=mesh, in_specs=in_specs,
        out_specs=(weight, weight), check_vma=False)
```

```python
import functools

import jax
import jax.numpy as jnp
from jax import lax
from jax.experimental import pallas as pl
from jax.experimental.pallas import tpu as pltpu
from jax.sharding import PartitionSpec as P

GROUP = 4
EPSILON = 1e-06
F32 = jnp.float32
BF16 = jnp.bfloat16
MESH = pl.DeviceIdType.MESH


def dot(a, b, a_dim, b_dim):
    return lax.dot_general(a, b, (((a_dim,), (b_dim,)), ((), ())), preferred_element_type=F32)


def kernel(
    sizes,
    saved, cot, routes, wg, wu, wd,
    out_gate, out_up,
    weights, head, place, unit_send, unit_full, grad_in, grad_send, grad_full,
    gate_f, up_f, gate_grad, up_grad, part, part_recv, middle, sums, sums_recv, grad_out,
    out_send, out_recv, early,
    w_s, w_r, h_s, h_r, u1_s, u1_r, u2_s, u2_r, g1_s, g1_r, g2_s, g2_r,
    a_s, a_r, b_s, b_r, x_s, x_r, o_s, o_r,
):
    sections, experts, n_dp, chunks, rows, tok, width = sizes
    sec = lax.axis_index("pipe")
    here = lax.axis_index("expert")
    core = lax.axis_index("dp")
    e_me = here // GROUP
    q_me = here % GROUP
    last = sections - 1
    half = width // n_dp

    def copy(src, dst, s_sem, r_sem, where):
        return pltpu.make_async_remote_copy(
            src_ref=src, dst_ref=dst, send_sem=s_sem, recv_sem=r_sem,
            device_id=where, device_id_type=MESH)

    def peer(step):
        e = (e_me + step) % experts
        return e, {"expert": e * GROUP + q_me}

    q_y = q_me + 1 - 2 * (q_me % 2)
    q_z = (q_me + 2) % GROUP
    q_far = GROUP - 1 - q_me
    to_y = {"expert": e_me * GROUP + q_y}
    to_z = {"expert": e_me * GROUP + q_z}
    cut = max(128, width * 3 // 4 // 128 * 128)
    major, minor = pl.ds(0, cut), pl.ds(cut, width - cut)

    def other(step):
        c = (core + step) % n_dp
        return c, {"dp": c}

    barrier = pltpu.get_barrier_semaphore()
    friends = [peer(i)[1] for i in range(1, experts)] + [to_y, to_z]
    friends += [other(i)[1] for i in range(1, n_dp)]
    friends += [{"pipe": (sec + i) % sections} for i in range(1, sections)]
    for friend in friends:
        pl.semaphore_signal(barrier, inc=1, device_id=friend, device_id_type=MESH)
    pl.semaphore_wait(barrier, len(friends))

    def head_copy():
        return copy(cot, head.at[sec], h_s.at[0], h_r.at[sec], {"pipe": sections - 1 + 0 * sec})

    @pl.when(sec != last)
    def _():
        head_copy().start()

    def scale_of(c):
        x = saved[pl.ds(c * tok, tok), :].astype(F32)
        scale = lax.rsqrt(jnp.mean(x * x, axis=1, keepdims=True) + EPSILON)
        return x * scale, scale

    def spread_one(c, rows_b, send, full, s_sem, r_sem):
        ordered = dot(place[c], rows_b, 0, 0).astype(BF16)
        for e in range(experts):
            send[c, e] = ordered[e * rows:(e + 1) * rows]
        for i in range(1, experts):
            e, where = peer(i)
            copy(send.at[c, e], full.at[c, q_me, e_me], s_sem.at[c, e], r_sem.at[c, e_me], where).start()
        full[c, q_me, e_me] = send[c, e_me]

    def spread_two(c, send, full, s1, r1, s2, r2):
        for i in range(1, experts):
            e, where = peer(i)
            copy(send.at[c, e], full.at[c, q_me, e], s1.at[c, e], r1.at[c, e], where).wait_recv()
        group_copy(c, full, s2, r2, 0, q_me).start()
        group_copy(c, full, s2, r2, 1, q_me).start()

    def group_copy(c, full, s2, r2, kind, q):
        ref = full.at[c, q]
        if kind >= 2:
            ref = ref.at[:, :, major if kind == 2 else minor]
        return copy(ref, ref, s2.at[c, kind], r2.at[c, kind], to_z if kind % 2 else to_y)

    def relay(c, full, s2, r2):
        group_copy(c, full, s2, r2, 1, q_z).wait_recv()
        group_copy(c, full, s2, r2, 2, q_z).start()
        group_copy(c, full, s2, r2, 0, q_y).wait_recv()
        group_copy(c, full, s2, r2, 3, q_y).start()

    def spread_end(c, full, s2, r2):
        group_copy(c, full, s2, r2, 2, q_far).wait_recv()
        group_copy(c, full, s2, r2, 3, q_far).wait_recv()

    for c in range(chunks):
        chosen = routes[pl.ds(c * tok, tok), :]
        lanes = max(128, experts)
        onehot = (chosen == lax.broadcasted_iota(jnp.int32, (tok, lanes), 1)).astype(F32)
        below = (lax.broadcasted_iota(jnp.int32, (tok, tok), 1)
                 < lax.broadcasted_iota(jnp.int32, (tok, tok), 0)).astype(F32)
        ahead = dot(below.astype(BF16), onehot.astype(BF16), 1, 0)
        rank = jnp.sum(ahead * onehot, axis=1, keepdims=True)
        slot = chosen * rows + rank.astype(jnp.int32)
        place[c] = (slot == lax.broadcasted_iota(jnp.int32, (tok, tok), 1)).astype(F32).astype(BF16)
        unit, _ = scale_of(c)
        spread_one(c, unit.astype(BF16), unit_send, unit_full, u1_s, u1_r)

    for k, ref in enumerate((wg, wu, wd)):
        for i in range(1, n_dp):
            d, where = other(i)
            copy(ref, weights.at[k, core], w_s.at[k, d], w_r.at[k, core], where).start()
        weights[k, core] = ref[...]

    @pl.when(sec == last)
    def _():
        cols = width // sections
        for s in range(last):
            copy(cot, head.at[s], h_s.at[0], h_r.at[s], {"pipe": s}).wait_recv()
        for c in range(chunks):
            for s in range(sections):
                source = cot if s == last else head.at[s]
                grad_in[c, :, s * cols:(s + 1) * cols] = source[c * tok:(c + 1) * tok, :]
            spread_one(c, grad_in[c], grad_send, grad_full, g1_s, g1_r)

    for c in range(chunks):
        spread_two(c, unit_send, unit_full, u1_s, u1_r, u2_s, u2_r)

    for c in range(chunks):
        relay(c, unit_full, u2_s, u2_r)

        @pl.when(sec == last)
        def _():
            spread_two(c, grad_send, grad_full, g1_s, g1_r, g2_s, g2_r)

    for k, ref in enumerate((wg, wu, wd)):
        for i in range(1, n_dp):
            d, where = other(i)
            copy(ref, weights.at[k, d], w_s.at[k, d], w_r.at[k, d], where).wait_recv()

    per_block = GROUP if GROUP * experts * rows <= 256 else 1
    blocks = [(first, per_block) for first in range(0, GROUP, per_block)]
    block_rows = per_block * experts * rows

    def rows_of(full, c, first, count):
        return full[c, first:first + count].reshape(block_rows, width)

    def project(x, k):
        total = dot(x[:, :half], weights[k, 0], 1, 1)
        for d in range(1, n_dp):
            total = total + dot(x[:, d * half:(d + 1) * half], weights[k, d], 1, 1)
        return total

    for c in range(chunks):
        spread_end(c, unit_full, u2_s, u2_r)
        for first, count in blocks:
            x = rows_of(unit_full, c, first, count)
            at = pl.ds(c * GROUP * experts * rows + first * experts * rows, block_rows)
            gate_f[at, :] = project(x, 0)
            up_f[at, :] = project(x, 1)

    def backward(c):
        spread_end(c, grad_full, g2_s, g2_r)
        for first, count in blocks:
            at = pl.ds(c * GROUP * experts * rows + first * experts * rows, block_rows)
            hidden_grad = project(rows_of(grad_full, c, first, count), 2)
            gate = gate_f[at, :]
            up = up_f[at, :]
            sig = jax.nn.sigmoid(gate)
            gate_g = (hidden_grad * up * sig * (1.0 + gate * (1.0 - sig))).astype(BF16)
            up_g = (hidden_grad * gate * sig).astype(BF16)
            gate_grad[at, :] = gate_g
            up_grad[at, :] = up_g

            @pl.when(sec > 0)
            def _():
                for d in range(n_dp):
                    value = dot(gate_g, weights[0, d], 1, 0) + dot(up_g, weights[1, d], 1, 0)
                    part[c, first:first + count, :, :, d * half:(d + 1) * half] = (
                        value.astype(BF16).reshape(count, experts, rows, half))

        @pl.when(sec > 0)
        def _():
            for kind in (1, 3, 0, 2):
                back_copy(c, kind).start()

    def back_copy(c, kind):
        cols = major if kind in (0, 1, 4) else minor
        if kind < 4:
            q = (q_y, q_far, q_z, q_far)[kind]
            src, slot, where = part.at[c, q], kind % 2, (to_y if kind < 2 else to_z)
        else:
            src, slot, where = middle.at[c], 2, (to_z if kind == 4 else to_y)
        return copy(src.at[:, :, cols], part_recv.at[c, slot].at[:, :, cols],
                    a_s.at[c, kind], a_r.at[c, kind], where)

    def pair(c):
        for kind, cols, q in ((1, slice(0, cut), q_z), (3, slice(cut, width), q_y)):
            back_copy(c, kind).wait_recv()
            middle[c, :, :, cols] = (
                part[c, q, :, :, cols].astype(F32) + part_recv[c, 1, :, :, cols].astype(F32)
            ).astype(BF16)
            back_copy(c, 4 if kind == 1 else 5).start()

    def fold(c):
        for kind in (0, 2, 4, 5):
            back_copy(c, kind).wait_recv()
        total = part[c, q_me].astype(F32) + part_recv[c, 0].astype(F32) + part_recv[c, 2].astype(F32)
        sums[c] = total.astype(BF16)
        for i in range(1, experts):
            e, where = peer(i)
            copy(sums.at[c, e], sums_recv.at[c, e_me], b_s.at[c, e], b_r.at[c, e_me], where).start()
        sums_recv[c, e_me] = sums[c, e_me]

    def x_copy(c):
        return copy(grad_out.at[c], grad_in.at[c], x_s.at[c], x_r.at[c],
                    {"pipe": (sec + sections - 1) % sections})

    def finish(c):
        for i in range(1, experts):
            e, where = peer(i)
            copy(sums.at[c, e], sums_recv.at[c, e], b_s.at[c, e], b_r.at[c, e], where).wait_recv()
        unit_g = dot(place[c], sums_recv[c].reshape(tok, width), 1, 0)
        unit, scale = scale_of(c)
        norm = scale * (unit_g - unit * jnp.mean(unit_g * unit, axis=1, keepdims=True))
        grad_out[c] = (grad_in[c].astype(F32) + norm).astype(BF16)
        x_copy(c).start()

    chunk_rows = GROUP * experts * rows

    def outer(k, d, first, count):
        left = (gate_grad, up_grad)[k][pl.ds(first * chunk_rows, count * chunk_rows), :]
        right = unit_full[first:first + count, :, :, :, d * half:(d + 1) * half]
        return dot(left, right.reshape(count * chunk_rows, half), 0, 0)

    def sum_early():
        for k in range(2):
            for d in range(n_dp):
                early[k, d] = outer(k, d, 0, chunks - 1)

    @pl.when(sec == last)
    def _():
        relay(0, grad_full, g2_s, g2_r)

    for t in range(chunks + 3):
        if t < chunks:
            if t > 0 and t == chunks - 1:
                pl.when(sec == 0)(sum_early)

            if t + 1 < chunks:
                @pl.when(sec == last)
                def _():
                    relay(t + 1, grad_full, g2_s, g2_r)

            @pl.when(sec != last)
            def _():
                x_copy(t).wait_recv()
                spread_one(t, grad_in[t], grad_send, grad_full, g1_s, g1_r)
                spread_two(t, grad_send, grad_full, g1_s, g1_r, g2_s, g2_r)
                relay(t, grad_full, g2_s, g2_r)

            backward(t)

        @pl.when(sec > 0)
        def _():
            if 0 <= t - 1 < chunks:
                pair(t - 1)
            if 0 <= t - 2 < chunks:
                fold(t - 2)
            if 0 <= t - 3 < chunks:
                finish(t - 3)

    if chunks > 1:
        pl.when(sec > 0)(sum_early)

    def o_copy(k, i, mine):
        d, where = other(i)
        return copy(out_send.at[k, d], out_recv.at[k, core if mine else d],
                    o_s.at[k, d], o_r.at[k, core if mine else d], where)

    for k in range(2):
        for d in range(n_dp):
            value = outer(k, d, chunks - 1, 1)
            if chunks > 1:
                value = value + early[k, d]
            out_send[k, d] = value.astype(BF16)
        for i in range(1, n_dp):
            o_copy(k, i, True).start()
    for k, out in enumerate((out_gate, out_up)):
        total = out_send[k, core].astype(F32)
        for i in range(1, n_dp):
            d, _ = other(i)
            o_copy(k, i, False).wait_recv()
            total = total + out_recv[k, d].astype(F32)
        out[...] = total.astype(BF16)

    for k, ref in enumerate((wg, wu, wd)):
        for i in range(1, n_dp):
            d, where = other(i)
            copy(ref, weights.at[k, d], w_s.at[k, d], w_r.at[k, d], where).wait_send()
    for k in range(2):
        for i in range(1, n_dp):
            o_copy(k, i, True).wait_send()

    @pl.when(sec != last)
    def _():
        head_copy().wait_send()

    for c in range(chunks):
        for i in range(1, experts):
            e, where = peer(i)
            copy(unit_send.at[c, e], unit_full.at[c, q_me, e], u1_s.at[c, e], u1_r.at[c, e], where).wait_send()
            copy(grad_send.at[c, e], grad_full.at[c, q_me, e], g1_s.at[c, e], g1_r.at[c, e], where).wait_send()
        for kind, q in enumerate((q_me, q_me, q_z, q_y)):
            group_copy(c, unit_full, u2_s, u2_r, kind, q).wait_send()
            group_copy(c, grad_full, g2_s, g2_r, kind, q).wait_send()

    @pl.when(sec > 0)
    def _():
        for c in range(chunks):
            for kind in range(6):
                back_copy(c, kind).wait_send()
            for i in range(1, experts):
                e, where = peer(i)
                copy(sums.at[c, e], sums_recv.at[c, e], b_s.at[c, e], b_r.at[c, e], where).wait_send()
            x_copy(c).wait_send()


def shards(mesh, saved, cotangent, routes, w_gate, w_up, w_down):
    sections, spots, n_dp = mesh.shape["pipe"], mesh.shape["expert"], mesh.shape["dp"]
    experts = spots // GROUP
    tokens, width = saved.shape[2], saved.shape[3]
    hidden, half = w_gate.shape[2], w_gate.shape[3]
    chunks = max(1, min(4, tokens // (experts * 16)))
    tok = tokens // chunks
    rows = tok // experts
    sizes = (sections, experts, n_dp, chunks, rows, tok, width)
    all_rows = chunks * GROUP * experts * rows
    full = (chunks, GROUP, experts, rows, width)
    own = (chunks, experts, rows, width)
    dma = pltpu.SemaphoreType.DMA
    vm = pltpu.VMEM
    result = jax.ShapeDtypeStruct((hidden, half), BF16)
    scratch = [
        vm((3, n_dp, hidden, half), BF16),
        vm((sections,) + cotangent.shape, BF16),
        vm((chunks, tok, tok), BF16),
        vm(own, BF16), vm(full, BF16),
        vm((chunks, tok, width), BF16),
        vm(own, BF16), vm(full, BF16),
        vm((all_rows, hidden), F32), vm((all_rows, hidden), F32),
        vm((all_rows, hidden), BF16), vm((all_rows, hidden), BF16),
        vm(full, BF16), vm((chunks, 3) + own[1:], BF16), vm(own, BF16),
        vm(own, BF16), vm(own, BF16),
        vm((chunks, tok, width), BF16),
        vm((2, n_dp, hidden, half), BF16), vm((2, n_dp, hidden, half), BF16),
        vm((2, n_dp, hidden, half), F32),
        dma((3, n_dp)), dma((3, n_dp)),
        dma((1,)), dma((sections,)),
        dma((chunks, experts)), dma((chunks, experts)),
        dma((chunks, GROUP)), dma((chunks, GROUP)),
        dma((chunks, experts)), dma((chunks, experts)),
        dma((chunks, GROUP)), dma((chunks, GROUP)),
        dma((chunks, 6)), dma((chunks, 6)),
        dma((chunks, experts)), dma((chunks, experts)),
        dma((chunks,)), dma((chunks,)),
        dma((2, n_dp)), dma((2, n_dp)),
    ]
    flops = 14 * all_rows * hidden * width
    gate, up = pl.pallas_call(
        functools.partial(kernel, sizes),
        out_shape=(result, result),
        in_specs=[pl.BlockSpec(memory_space=pltpu.VMEM)] * 6,
        out_specs=[pl.BlockSpec(memory_space=pltpu.VMEM)] * 2,
        scratch_shapes=scratch,
        compiler_params=pltpu.CompilerParams(
            collective_id=0, has_side_effects=True, vmem_limit_bytes=52 * 1024 * 1024),
        cost_estimate=pl.CostEstimate(
            flops=flops, bytes_accessed=12 * hidden * half, transcendentals=all_rows * hidden),
    )(saved[0, 0], cotangent, routes[0, 0], w_gate[0, 0], w_up[0, 0], w_down[0, 0])
    return gate[None, None], up[None, None]


def solution(mesh):
    weight = P(None, "pipe", "expert", "dp")
    rows = P(None, "pipe", ("expert", "dp"), None)
    in_specs = (rows, P(("expert", "dp"), "pipe"), rows, weight, weight, weight)
    return jax.shard_map(
        functools.partial(shards, mesh), mesh=mesh, in_specs=in_specs,
        out_specs=(weight, weight), check_vma=False)
```

```python
import functools

import jax
import jax.numpy as jnp
from jax import lax
from jax.experimental import pallas as pl
from jax.experimental.pallas import tpu as pltpu
from jax.sharding import PartitionSpec as P

GROUP = 4
EPSILON = 1e-06
F32 = jnp.float32
BF16 = jnp.bfloat16
MESH = pl.DeviceIdType.MESH


def dot(a, b, a_dim, b_dim):
    return lax.dot_general(a, b, (((a_dim,), (b_dim,)), ((), ())), preferred_element_type=F32)


def kernel(
    sizes,
    saved, cot, routes, wg, wu, wd,
    out_gate, out_up,
    weights, head, place, unit_send, unit_full, grad_in, grad_send, grad_full,
    gate_f, up_f, gate_grad, up_grad, part, part_recv, middle, sums, sums_recv, grad_out,
    out_send, out_recv, early,
    w_s, w_r, h_s, h_r, u1_s, u1_r, u2_s, u2_r, g1_s, g1_r, g2_s, g2_r,
    a_s, a_r, b_s, b_r, x_s, x_r, o_s, o_r,
):
    sections, experts, n_dp, chunks, rows, tok, width = sizes
    sec = lax.axis_index("pipe")
    here = lax.axis_index("expert")
    core = lax.axis_index("dp")
    e_me = here // GROUP
    q_me = here % GROUP
    last = sections - 1
    half = width // n_dp

    def copy(src, dst, s_sem, r_sem, where):
        return pltpu.make_async_remote_copy(
            src_ref=src, dst_ref=dst, send_sem=s_sem, recv_sem=r_sem,
            device_id=where, device_id_type=MESH)

    def peer(step):
        e = (e_me + step) % experts
        return e, {"expert": e * GROUP + q_me}

    q_y = q_me + 1 - 2 * (q_me % 2)
    q_z = (q_me + 2) % GROUP
    q_far = GROUP - 1 - q_me
    to_y = {"expert": e_me * GROUP + q_y}
    to_z = {"expert": e_me * GROUP + q_z}
    cut = max(128, width * 3 // 4 // 128 * 128)
    major, minor = pl.ds(0, cut), pl.ds(cut, width - cut)

    def other(step):
        c = (core + step) % n_dp
        return c, {"dp": c}

    barrier = pltpu.get_barrier_semaphore()
    friends = [peer(i)[1] for i in range(1, experts)] + [to_y, to_z]
    friends += [other(i)[1] for i in range(1, n_dp)]
    friends += [{"pipe": (sec + i) % sections} for i in range(1, sections)]
    for friend in friends:
        pl.semaphore_signal(barrier, inc=1, device_id=friend, device_id_type=MESH)
    pl.semaphore_wait(barrier, len(friends))

    def head_copy():
        return copy(cot, head.at[sec], h_s.at[0], h_r.at[sec], {"pipe": sections - 1 + 0 * sec})

    @pl.when(sec != last)
    def _():
        head_copy().start()

    def scale_of(c):
        x = saved[pl.ds(c * tok, tok), :].astype(F32)
        scale = lax.rsqrt(jnp.mean(x * x, axis=1, keepdims=True) + EPSILON)
        return x * scale, scale

    def spread_one(c, rows_b, send, full, s_sem, r_sem):
        ordered = dot(place[c], rows_b, 0, 0).astype(BF16)
        for e in range(experts):
            send[c, e] = ordered[e * rows:(e + 1) * rows]
        for i in range(1, experts):
            e, where = peer(i)
            copy(send.at[c, e], full.at[c, q_me, e_me], s_sem.at[c, e], r_sem.at[c, e_me], where).start()
        full[c, q_me, e_me] = send[c, e_me]

    def spread_two(c, send, full, s1, r1, s2, r2):
        for i in range(1, experts):
            e, where = peer(i)
            copy(send.at[c, e], full.at[c, q_me, e], s1.at[c, e], r1.at[c, e], where).wait_recv()
        group_copy(c, full, s2, r2, 0, q_me).start()
        group_copy(c, full, s2, r2, 1, q_me).start()

    def group_copy(c, full, s2, r2, kind, q):
        ref = full.at[c, q]
        if kind >= 2:
            ref = ref.at[:, :, major if kind == 2 else minor]
        return copy(ref, ref, s2.at[c, kind], r2.at[c, kind], to_z if kind % 2 else to_y)

    def relay(c, full, s2, r2):
        group_copy(c, full, s2, r2, 1, q_z).wait_recv()
        group_copy(c, full, s2, r2, 2, q_z).start()
        group_copy(c, full, s2, r2, 0, q_y).wait_recv()
        group_copy(c, full, s2, r2, 3, q_y).start()

    def spread_end(c, full, s2, r2):
        group_copy(c, full, s2, r2, 2, q_far).wait_recv()
        group_copy(c, full, s2, r2, 3, q_far).wait_recv()

    for c in range(chunks):
        chosen = routes[pl.ds(c * tok, tok), :]
        lanes = max(128, experts)
        onehot = (chosen == lax.broadcasted_iota(jnp.int32, (tok, lanes), 1)).astype(F32)
        below = (lax.broadcasted_iota(jnp.int32, (tok, tok), 1)
                 < lax.broadcasted_iota(jnp.int32, (tok, tok), 0)).astype(F32)
        ahead = dot(below.astype(BF16), onehot.astype(BF16), 1, 0)
        rank = jnp.sum(ahead * onehot, axis=1, keepdims=True)
        slot = chosen * rows + rank.astype(jnp.int32)
        place[c] = (slot == lax.broadcasted_iota(jnp.int32, (tok, tok), 1)).astype(F32).astype(BF16)
        unit, _ = scale_of(c)
        spread_one(c, unit.astype(BF16), unit_send, unit_full, u1_s, u1_r)

    for k, ref in enumerate((wg, wu, wd)):
        for i in range(1, n_dp):
            d, where = other(i)
            copy(ref, weights.at[k, core], w_s.at[k, d], w_r.at[k, core], where).start()
        weights[k, core] = ref[...]

    @pl.when(sec == last)
    def _():
        cols = width // sections
        for s in range(last):
            copy(cot, head.at[s], h_s.at[0], h_r.at[s], {"pipe": s}).wait_recv()
        for c in range(chunks):
            for s in range(sections):
                source = cot if s == last else head.at[s]
                grad_in[c, :, s * cols:(s + 1) * cols] = source[c * tok:(c + 1) * tok, :]
            spread_one(c, grad_in[c], grad_send, grad_full, g1_s, g1_r)

    for c in range(chunks):
        spread_two(c, unit_send, unit_full, u1_s, u1_r, u2_s, u2_r)

    for c in range(chunks):
        relay(c, unit_full, u2_s, u2_r)

        @pl.when(sec == last)
        def _():
            spread_two(c, grad_send, grad_full, g1_s, g1_r, g2_s, g2_r)

    for k, ref in enumerate((wg, wu, wd)):
        for i in range(1, n_dp):
            d, where = other(i)
            copy(ref, weights.at[k, d], w_s.at[k, d], w_r.at[k, d], where).wait_recv()

    per_block = GROUP if GROUP * experts * rows <= 256 else 1
    blocks = [(first, per_block) for first in range(0, GROUP, per_block)]
    block_rows = per_block * experts * rows

    def rows_of(full, c, first, count):
        return full[c, first:first + count].reshape(block_rows, width)

    def project(x, k):
        total = dot(x[:, :half], weights[k, 0], 1, 1)
        for d in range(1, n_dp):
            total = total + dot(x[:, d * half:(d + 1) * half], weights[k, d], 1, 1)
        return total

    for c in range(chunks):
        spread_end(c, unit_full, u2_s, u2_r)
        for first, count in blocks:
            x = rows_of(unit_full, c, first, count)
            at = pl.ds(c * GROUP * experts * rows + first * experts * rows, block_rows)
            gate_f[at, :] = project(x, 0)
            up_f[at, :] = project(x, 1)

    def backward(c):
        spread_end(c, grad_full, g2_s, g2_r)
        for first, count in blocks:
            at = pl.ds(c * GROUP * experts * rows + first * experts * rows, block_rows)
            hidden_grad = project(rows_of(grad_full, c, first, count), 2)
            gate = gate_f[at, :]
            up = up_f[at, :]
            sig = jax.nn.sigmoid(gate)
            gate_g = (hidden_grad * up * sig * (1.0 + gate * (1.0 - sig))).astype(BF16)
            up_g = (hidden_grad * gate * sig).astype(BF16)
            gate_grad[at, :] = gate_g
            up_grad[at, :] = up_g

            @pl.when(sec > 0)
            def _():
                for d in range(n_dp):
                    value = dot(gate_g, weights[0, d], 1, 0) + dot(up_g, weights[1, d], 1, 0)
                    part[c, first:first + count, :, :, d * half:(d + 1) * half] = (
                        value.astype(BF16).reshape(count, experts, rows, half))

        @pl.when(sec > 0)
        def _():
            for kind in (1, 3, 0, 2):
                back_copy(c, kind).start()

    def back_copy(c, kind):
        cols = major if kind in (0, 1, 4) else minor
        if kind < 4:
            q = (q_y, q_far, q_z, q_far)[kind]
            src, slot, where = part.at[c, q], kind % 2, (to_y if kind < 2 else to_z)
        else:
            src, slot, where = middle.at[c], 2, (to_z if kind == 4 else to_y)
        return copy(src.at[:, :, cols], part_recv.at[c, slot].at[:, :, cols],
                    a_s.at[c, kind], a_r.at[c, kind], where)

    def pair(c):
        for kind, cols, q in ((1, slice(0, cut), q_z), (3, slice(cut, width), q_y)):
            back_copy(c, kind).wait_recv()
            middle[c, :, :, cols] = (
                part[c, q, :, :, cols].astype(F32) + part_recv[c, 1, :, :, cols].astype(F32)
            ).astype(BF16)
            back_copy(c, 4 if kind == 1 else 5).start()

    def fold(c):
        for kind in (0, 2, 4, 5):
            back_copy(c, kind).wait_recv()
        total = part[c, q_me].astype(F32) + part_recv[c, 0].astype(F32) + part_recv[c, 2].astype(F32)
        sums[c] = total.astype(BF16)
        for i in range(1, experts):
            e, where = peer(i)
            copy(sums.at[c, e], sums_recv.at[c, e_me], b_s.at[c, e], b_r.at[c, e_me], where).start()
        sums_recv[c, e_me] = sums[c, e_me]

    def x_copy(c):
        return copy(grad_out.at[c], grad_in.at[c], x_s.at[c], x_r.at[c],
                    {"pipe": (sec + sections - 1) % sections})

    def finish(c):
        for i in range(1, experts):
            e, where = peer(i)
            copy(sums.at[c, e], sums_recv.at[c, e], b_s.at[c, e], b_r.at[c, e], where).wait_recv()
        unit_g = dot(place[c], sums_recv[c].reshape(tok, width), 1, 0)
        unit, scale = scale_of(c)
        norm = scale * (unit_g - unit * jnp.mean(unit_g * unit, axis=1, keepdims=True))
        grad_out[c] = (grad_in[c].astype(F32) + norm).astype(BF16)
        x_copy(c).start()

    chunk_rows = GROUP * experts * rows

    def outer(k, d, first, count):
        left = (gate_grad, up_grad)[k][pl.ds(first * chunk_rows, count * chunk_rows), :]
        right = unit_full[first:first + count, :, :, :, pl.ds(pl.multiple_of(d * half, 128), half)]
        return dot(left, right.reshape(count * chunk_rows, half), 0, 0)

    def sum_early():
        for k in range(2):
            for d in range(n_dp):
                early[k, d] = outer(k, d, 0, chunks - 1)

    for t in range(-3, chunks + 3):
        @pl.when(sec != last)
        def _():
            if 0 <= t + 3 < chunks:
                x_copy(t + 3).wait_recv()
                spread_one(t + 3, grad_in[t + 3], grad_send, grad_full, g1_s, g1_r)
            if 0 <= t + 2 < chunks:
                spread_two(t + 2, grad_send, grad_full, g1_s, g1_r, g2_s, g2_r)

        if 0 <= t + 1 < chunks:
            relay(t + 1, grad_full, g2_s, g2_r)
        if 0 <= t < chunks:
            if t > 0 and t == chunks - 1:
                pl.when(sec == 0)(sum_early)
            backward(t)

        @pl.when(sec > 0)
        def _():
            if 0 <= t - 1 < chunks:
                pair(t - 1)
            if 0 <= t - 2 < chunks:
                fold(t - 2)
            if 0 <= t - 3 < chunks:
                finish(t - 3)

    if chunks > 1:
        pl.when(sec > 0)(sum_early)

    def o_copy(k, i, mine):
        d, where = other(i)
        return copy(out_send.at[k, d], out_recv.at[k, core if mine else d],
                    o_s.at[k, d], o_r.at[k, core if mine else d], where)

    def outer_all(k, d):
        value = outer(k, d, chunks - 1, 1)
        if chunks > 1:
            value = value + early[k, d]
        out_send[k, d] = value.astype(BF16)

    for k in range(2):
        for i in range(1, n_dp):
            outer_all(k, other(i)[0])
            o_copy(k, i, True).start()
    for k in range(2):
        outer_all(k, core)
    for k, out in enumerate((out_gate, out_up)):
        total = out_send[k, core].astype(F32)
        for i in range(1, n_dp):
            d, _ = other(i)
            o_copy(k, i, False).wait_recv()
            total = total + out_recv[k, d].astype(F32)
        out[...] = total.astype(BF16)

    for k, ref in enumerate((wg, wu, wd)):
        for i in range(1, n_dp):
            d, where = other(i)
            copy(ref, weights.at[k, d], w_s.at[k, d], w_r.at[k, d], where).wait_send()
    for k in range(2):
        for i in range(1, n_dp):
            o_copy(k, i, True).wait_send()

    @pl.when(sec != last)
    def _():
        head_copy().wait_send()

    for c in range(chunks):
        for i in range(1, experts):
            e, where = peer(i)
            copy(unit_send.at[c, e], unit_full.at[c, q_me, e], u1_s.at[c, e], u1_r.at[c, e], where).wait_send()
            copy(grad_send.at[c, e], grad_full.at[c, q_me, e], g1_s.at[c, e], g1_r.at[c, e], where).wait_send()
        for kind, q in enumerate((q_me, q_me, q_z, q_y)):
            group_copy(c, unit_full, u2_s, u2_r, kind, q).wait_send()
            group_copy(c, grad_full, g2_s, g2_r, kind, q).wait_send()

    @pl.when(sec > 0)
    def _():
        for c in range(chunks):
            for kind in range(6):
                back_copy(c, kind).wait_send()
            for i in range(1, experts):
                e, where = peer(i)
                copy(sums.at[c, e], sums_recv.at[c, e], b_s.at[c, e], b_r.at[c, e], where).wait_send()
            x_copy(c).wait_send()


def shards(mesh, saved, cotangent, routes, w_gate, w_up, w_down):
    sections, spots, n_dp = mesh.shape["pipe"], mesh.shape["expert"], mesh.shape["dp"]
    experts = spots // GROUP
    tokens, width = saved.shape[2], saved.shape[3]
    hidden, half = w_gate.shape[2], w_gate.shape[3]
    chunks = max(1, min(4, tokens // (experts * 16)))
    tok = tokens // chunks
    rows = tok // experts
    sizes = (sections, experts, n_dp, chunks, rows, tok, width)
    all_rows = chunks * GROUP * experts * rows
    full = (chunks, GROUP, experts, rows, width)
    own = (chunks, experts, rows, width)
    dma = pltpu.SemaphoreType.DMA
    vm = pltpu.VMEM
    result = jax.ShapeDtypeStruct((hidden, half), BF16)
    scratch = [
        vm((3, n_dp, hidden, half), BF16),
        vm((sections,) + cotangent.shape, BF16),
        vm((chunks, tok, tok), BF16),
        vm(own, BF16), vm(full, BF16),
        vm((chunks, tok, width), BF16),
        vm(own, BF16), vm(full, BF16),
        vm((all_rows, hidden), F32), vm((all_rows, hidden), F32),
        vm((all_rows, hidden), BF16), vm((all_rows, hidden), BF16),
        vm(full, BF16), vm((chunks, 3) + own[1:], BF16), vm(own, BF16),
        vm(own, BF16), vm(own, BF16),
        vm((chunks, tok, width), BF16),
        vm((2, n_dp, hidden, half), BF16), vm((2, n_dp, hidden, half), BF16),
        vm((2, n_dp, hidden, half), F32),
        dma((3, n_dp)), dma((3, n_dp)),
        dma((1,)), dma((sections,)),
        dma((chunks, experts)), dma((chunks, experts)),
        dma((chunks, GROUP)), dma((chunks, GROUP)),
        dma((chunks, experts)), dma((chunks, experts)),
        dma((chunks, GROUP)), dma((chunks, GROUP)),
        dma((chunks, 6)), dma((chunks, 6)),
        dma((chunks, experts)), dma((chunks, experts)),
        dma((chunks,)), dma((chunks,)),
        dma((2, n_dp)), dma((2, n_dp)),
    ]
    flops = 14 * all_rows * hidden * width
    gate, up = pl.pallas_call(
        functools.partial(kernel, sizes),
        out_shape=(result, result),
        in_specs=[pl.BlockSpec(memory_space=pltpu.VMEM)] * 6,
        out_specs=[pl.BlockSpec(memory_space=pltpu.VMEM)] * 2,
        scratch_shapes=scratch,
        compiler_params=pltpu.CompilerParams(
            collective_id=0, has_side_effects=True, vmem_limit_bytes=52 * 1024 * 1024),
        cost_estimate=pl.CostEstimate(
            flops=flops, bytes_accessed=12 * hidden * half, transcendentals=all_rows * hidden),
    )(saved[0, 0], cotangent, routes[0, 0], w_gate[0, 0], w_up[0, 0], w_down[0, 0])
    return gate[None, None], up[None, None]


def solution(mesh):
    weight = P(None, "pipe", "expert", "dp")
    rows = P(None, "pipe", ("expert", "dp"), None)
    in_specs = (rows, P(("expert", "dp"), "pipe"), rows, weight, weight, weight)
    return jax.shard_map(
        functools.partial(shards, mesh), mesh=mesh, in_specs=in_specs,
        out_specs=(weight, weight), check_vma=False)
```

```python
import functools

import jax
import jax.numpy as jnp
from jax import lax
from jax.experimental import pallas as pl
from jax.experimental.pallas import tpu as pltpu
from jax.sharding import PartitionSpec as P

GROUP = 4
EPSILON = 1e-06
F32 = jnp.float32
BF16 = jnp.bfloat16
MESH = pl.DeviceIdType.MESH


def dot(a, b, a_dim, b_dim):
    return lax.dot_general(a, b, (((a_dim,), (b_dim,)), ((), ())), preferred_element_type=F32)


def kernel(
    sizes,
    saved, cot, routes, wg, wu, wd,
    out_gate, out_up,
    weights, head, place, unit_send, unit_full, grad_in, grad_send, grad_full,
    gate_f, up_f, gate_grad, up_grad, part, part_recv, middle, sums, sums_recv, grad_out,
    out_send, out_recv, early,
    w_s, w_r, h_s, h_r, u1_s, u1_r, u2_s, u2_r, g1_s, g1_r, g2_s, g2_r,
    a_s, a_r, b_s, b_r, x_s, x_r, o_s, o_r, l_s,
):
    sections, experts, n_dp, chunks, rows, tok, width = sizes
    sec = lax.axis_index("pipe")
    here = lax.axis_index("expert")
    core = lax.axis_index("dp")
    e_me = here // GROUP
    q_me = here % GROUP
    last = sections - 1
    half = width // n_dp

    def copy(src, dst, s_sem, r_sem, where):
        return pltpu.make_async_remote_copy(
            src_ref=src, dst_ref=dst, send_sem=s_sem, recv_sem=r_sem,
            device_id=where, device_id_type=MESH)

    def peer(step):
        e = (e_me + step) % experts
        return e, {"expert": e * GROUP + q_me}

    q_y = q_me + 1 - 2 * (q_me % 2)
    q_z = (q_me + 2) % GROUP
    q_far = GROUP - 1 - q_me
    to_y = {"expert": e_me * GROUP + q_y}
    to_z = {"expert": e_me * GROUP + q_z}
    cut = max(128, width * 3 // 4 // 128 * 128)
    major, minor = pl.ds(0, cut), pl.ds(cut, width - cut)

    def other(step):
        c = (core + step) % n_dp
        return c, {"dp": c}

    barrier = pltpu.get_barrier_semaphore()
    friends = [peer(i)[1] for i in range(1, experts)] + [to_y, to_z]
    friends += [other(i)[1] for i in range(1, n_dp)]
    friends += [{"pipe": (sec + i) % sections} for i in range(1, sections)]
    for friend in friends:
        pl.semaphore_signal(barrier, inc=1, device_id=friend, device_id_type=MESH)
    pl.semaphore_wait(barrier, len(friends))

    def head_copy():
        return copy(cot, head.at[sec], h_s.at[0], h_r.at[sec], {"pipe": sections - 1 + 0 * sec})

    @pl.when(sec != last)
    def _():
        head_copy().start()

    def scale_of(c):
        x = saved[pl.ds(c * tok, tok), :].astype(F32)
        scale = lax.rsqrt(jnp.mean(x * x, axis=1, keepdims=True) + EPSILON)
        return x * scale, scale

    def spread_one(c, rows_b, send, full, s_sem, r_sem):
        ordered = dot(place[c], rows_b, 0, 0).astype(BF16)
        for e in range(experts):
            send[c, e] = ordered[e * rows:(e + 1) * rows]
        for i in range(1, experts):
            e, where = peer(i)
            copy(send.at[c, e], full.at[c, q_me, e_me], s_sem.at[c, e], r_sem.at[c, e_me], where).start()
        full[c, q_me, e_me] = send[c, e_me]

    def spread_two(c, send, full, s1, r1, s2, r2):
        for i in range(1, experts):
            e, where = peer(i)
            copy(send.at[c, e], full.at[c, q_me, e], s1.at[c, e], r1.at[c, e], where).wait_recv()
        group_copy(c, full, s2, r2, 0, q_me).start()
        group_copy(c, full, s2, r2, 1, q_me).start()

    def group_copy(c, full, s2, r2, kind, q):
        ref = full.at[c, q]
        if kind >= 2:
            ref = ref.at[:, :, major if kind == 2 else minor]
        return copy(ref, ref, s2.at[c, kind], r2.at[c, kind], to_z if kind % 2 else to_y)

    def relay(c, full, s2, r2):
        group_copy(c, full, s2, r2, 1, q_z).wait_recv()
        group_copy(c, full, s2, r2, 2, q_z).start()
        group_copy(c, full, s2, r2, 0, q_y).wait_recv()
        group_copy(c, full, s2, r2, 3, q_y).start()

    def spread_end(c, full, s2, r2):
        group_copy(c, full, s2, r2, 2, q_far).wait_recv()
        group_copy(c, full, s2, r2, 3, q_far).wait_recv()

    for c in range(chunks):
        chosen = routes[pl.ds(c * tok, tok), :]
        lanes = max(128, experts)
        onehot = (chosen == lax.broadcasted_iota(jnp.int32, (tok, lanes), 1)).astype(F32)
        below = (lax.broadcasted_iota(jnp.int32, (tok, tok), 1)
                 < lax.broadcasted_iota(jnp.int32, (tok, tok), 0)).astype(F32)
        ahead = dot(below.astype(BF16), onehot.astype(BF16), 1, 0)
        rank = jnp.sum(ahead * onehot, axis=1, keepdims=True)
        slot = chosen * rows + rank.astype(jnp.int32)
        place[c] = (slot == lax.broadcasted_iota(jnp.int32, (tok, tok), 1)).astype(F32).astype(BF16)
        unit, _ = scale_of(c)
        spread_one(c, unit.astype(BF16), unit_send, unit_full, u1_s, u1_r)

    for k, ref in enumerate((wg, wu, wd)):
        for i in range(1, n_dp):
            d, where = other(i)
            copy(ref, weights.at[k, core], w_s.at[k, d], w_r.at[k, core], where).start()
        pltpu.make_async_copy(ref, weights.at[k, core], l_s.at[k]).start()

    @pl.when(sec == last)
    def _():
        cols = width // sections
        for s in range(last):
            copy(cot, head.at[s], h_s.at[0], h_r.at[s], {"pipe": s}).wait_recv()
        for c in range(chunks):
            for s in range(sections):
                source = cot if s == last else head.at[s]
                grad_in[c, :, s * cols:(s + 1) * cols] = source[c * tok:(c + 1) * tok, :]
            spread_one(c, grad_in[c], grad_send, grad_full, g1_s, g1_r)

    for c in range(chunks):
        spread_two(c, unit_send, unit_full, u1_s, u1_r, u2_s, u2_r)

    for c in range(chunks):
        relay(c, unit_full, u2_s, u2_r)

        @pl.when(sec == last)
        def _():
            spread_two(c, grad_send, grad_full, g1_s, g1_r, g2_s, g2_r)

    for k, ref in enumerate((wg, wu, wd)):
        for i in range(1, n_dp):
            d, where = other(i)
            copy(ref, weights.at[k, d], w_s.at[k, d], w_r.at[k, d], where).wait_recv()
        pltpu.make_async_copy(ref, weights.at[k, core], l_s.at[k]).wait()

    per_block = GROUP if GROUP * experts * rows <= 256 else 1
    blocks = [(first, per_block) for first in range(0, GROUP, per_block)]
    block_rows = per_block * experts * rows

    def rows_of(full, c, first, count):
        return full[c, first:first + count].reshape(block_rows, width)

    def project(x, k):
        total = dot(x[:, :half], weights[k, 0], 1, 1)
        for d in range(1, n_dp):
            total = total + dot(x[:, d * half:(d + 1) * half], weights[k, d], 1, 1)
        return total

    for c in range(chunks):
        spread_end(c, unit_full, u2_s, u2_r)
        for first, count in blocks:
            x = rows_of(unit_full, c, first, count)
            at = pl.ds(c * GROUP * experts * rows + first * experts * rows, block_rows)
            gate_f[at, :] = project(x, 0)
            up_f[at, :] = project(x, 1)

        @pl.when(sec == last)
        def _():
            relay(c, grad_full, g2_s, g2_r)

    def backward(c):
        spread_end(c, grad_full, g2_s, g2_r)
        for first, count in blocks:
            at = pl.ds(c * GROUP * experts * rows + first * experts * rows, block_rows)
            hidden_grad = project(rows_of(grad_full, c, first, count), 2)
            gate = gate_f[at, :]
            up = up_f[at, :]
            sig = jax.nn.sigmoid(gate)
            gate_g = (hidden_grad * up * sig * (1.0 + gate * (1.0 - sig))).astype(BF16)
            up_g = (hidden_grad * gate * sig).astype(BF16)
            gate_grad[at, :] = gate_g
            up_grad[at, :] = up_g

            @pl.when(sec > 0)
            def _():
                for d in range(n_dp):
                    value = dot(gate_g, weights[0, d], 1, 0) + dot(up_g, weights[1, d], 1, 0)
                    part[c, first:first + count, :, :, d * half:(d + 1) * half] = (
                        value.astype(BF16).reshape(count, experts, rows, half))

        @pl.when(sec > 0)
        def _():
            for kind in (1, 3, 0, 2):
                back_copy(c, kind).start()

    def back_copy(c, kind):
        cols = major if kind in (0, 1, 4) else minor
        if kind < 4:
            q = (q_y, q_far, q_z, q_far)[kind]
            src, slot, where = part.at[c, q], kind % 2, (to_y if kind < 2 else to_z)
        else:
            src, slot, where = middle.at[c], 2, (to_z if kind == 4 else to_y)
        return copy(src.at[:, :, cols], part_recv.at[c, slot].at[:, :, cols],
                    a_s.at[c, kind], a_r.at[c, kind], where)

    def pair(c):
        for kind, cols, q in ((1, slice(0, cut), q_z), (3, slice(cut, width), q_y)):
            back_copy(c, kind).wait_recv()
            middle[c, :, :, cols] = (
                part[c, q, :, :, cols].astype(F32) + part_recv[c, 1, :, :, cols].astype(F32)
            ).astype(BF16)
            back_copy(c, 4 if kind == 1 else 5).start()

    def fold(c):
        for kind in (0, 2, 4, 5):
            back_copy(c, kind).wait_recv()
        total = part[c, q_me].astype(F32) + part_recv[c, 0].astype(F32) + part_recv[c, 2].astype(F32)
        sums[c] = total.astype(BF16)
        for i in range(1, experts):
            e, where = peer(i)
            copy(sums.at[c, e], sums_recv.at[c, e_me], b_s.at[c, e], b_r.at[c, e_me], where).start()
        sums_recv[c, e_me] = sums[c, e_me]

    def x_copy(c):
        return copy(grad_out.at[c], grad_in.at[c], x_s.at[c], x_r.at[c],
                    {"pipe": (sec + sections - 1) % sections})

    def finish(c):
        for i in range(1, experts):
            e, where = peer(i)
            copy(sums.at[c, e], sums_recv.at[c, e], b_s.at[c, e], b_r.at[c, e], where).wait_recv()
        unit_g = dot(place[c], sums_recv[c].reshape(tok, width), 1, 0)
        unit, scale = scale_of(c)
        norm = scale * (unit_g - unit * jnp.mean(unit_g * unit, axis=1, keepdims=True))
        grad_out[c] = (grad_in[c].astype(F32) + norm).astype(BF16)
        x_copy(c).start()

    chunk_rows = GROUP * experts * rows

    def outer(k, d, first, count):
        left = (gate_grad, up_grad)[k][pl.ds(first * chunk_rows, count * chunk_rows), :]
        right = unit_full[first:first + count, :, :, :, pl.ds(pl.multiple_of(d * half, 128), half)]
        return dot(left, right.reshape(count * chunk_rows, half), 0, 0)

    def sum_early():
        for k in range(2):
            for d in range(n_dp):
                early[k, d] = outer(k, d, 0, chunks - 1)

    for t in range(-3, chunks + 3):
        @pl.when(sec != last)
        def _():
            if 0 <= t + 3 < chunks:
                x_copy(t + 3).wait_recv()
                spread_one(t + 3, grad_in[t + 3], grad_send, grad_full, g1_s, g1_r)
            if 0 <= t + 2 < chunks:
                spread_two(t + 2, grad_send, grad_full, g1_s, g1_r, g2_s, g2_r)
            if 0 <= t + 1 < chunks:
                relay(t + 1, grad_full, g2_s, g2_r)

        if 0 <= t < chunks:
            if t > 0 and t == chunks - 1:
                pl.when(sec == 0)(sum_early)
            backward(t)

        @pl.when(sec > 0)
        def _():
            if 0 <= t - 1 < chunks:
                pair(t - 1)
            if 0 <= t - 2 < chunks:
                fold(t - 2)
            if 0 <= t - 3 < chunks:
                finish(t - 3)

    if chunks > 1:
        pl.when(sec > 0)(sum_early)

    def o_copy(k, i, mine):
        d, where = other(i)
        return copy(out_send.at[k, d], out_recv.at[k, core if mine else d],
                    o_s.at[k, d], o_r.at[k, core if mine else d], where)

    def outer_all(k, d):
        value = outer(k, d, chunks - 1, 1)
        if chunks > 1:
            value = value + early[k, d]
        out_send[k, d] = value.astype(BF16)

    for k in range(2):
        for i in range(1, n_dp):
            outer_all(k, other(i)[0])
            o_copy(k, i, True).start()
    for k in range(2):
        outer_all(k, core)
    for k, out in enumerate((out_gate, out_up)):
        total = out_send[k, core].astype(F32)
        for i in range(1, n_dp):
            d, _ = other(i)
            o_copy(k, i, False).wait_recv()
            total = total + out_recv[k, d].astype(F32)
        out[...] = total.astype(BF16)

    for k, ref in enumerate((wg, wu, wd)):
        for i in range(1, n_dp):
            d, where = other(i)
            copy(ref, weights.at[k, d], w_s.at[k, d], w_r.at[k, d], where).wait_send()
    for k in range(2):
        for i in range(1, n_dp):
            o_copy(k, i, True).wait_send()

    @pl.when(sec != last)
    def _():
        head_copy().wait_send()

    for c in range(chunks):
        for i in range(1, experts):
            e, where = peer(i)
            copy(unit_send.at[c, e], unit_full.at[c, q_me, e], u1_s.at[c, e], u1_r.at[c, e], where).wait_send()
            copy(grad_send.at[c, e], grad_full.at[c, q_me, e], g1_s.at[c, e], g1_r.at[c, e], where).wait_send()
        for kind, q in enumerate((q_me, q_me, q_z, q_y)):
            group_copy(c, unit_full, u2_s, u2_r, kind, q).wait_send()
            group_copy(c, grad_full, g2_s, g2_r, kind, q).wait_send()

    @pl.when(sec > 0)
    def _():
        for c in range(chunks):
            for kind in range(6):
                back_copy(c, kind).wait_send()
            for i in range(1, experts):
                e, where = peer(i)
                copy(sums.at[c, e], sums_recv.at[c, e], b_s.at[c, e], b_r.at[c, e], where).wait_send()
            x_copy(c).wait_send()


def shards(mesh, saved, cotangent, routes, w_gate, w_up, w_down):
    sections, spots, n_dp = mesh.shape["pipe"], mesh.shape["expert"], mesh.shape["dp"]
    experts = spots // GROUP
    tokens, width = saved.shape[2], saved.shape[3]
    hidden, half = w_gate.shape[2], w_gate.shape[3]
    chunks = max(1, min(4, tokens // (experts * 16)))
    tok = tokens // chunks
    rows = tok // experts
    sizes = (sections, experts, n_dp, chunks, rows, tok, width)
    all_rows = chunks * GROUP * experts * rows
    full = (chunks, GROUP, experts, rows, width)
    own = (chunks, experts, rows, width)
    dma = pltpu.SemaphoreType.DMA
    vm = pltpu.VMEM
    result = jax.ShapeDtypeStruct((hidden, half), BF16)
    scratch = [
        vm((3, n_dp, hidden, half), BF16),
        vm((sections,) + cotangent.shape, BF16),
        vm((chunks, tok, tok), BF16),
        vm(own, BF16), vm(full, BF16),
        vm((chunks, tok, width), BF16),
        vm(own, BF16), vm(full, BF16),
        vm((all_rows, hidden), F32), vm((all_rows, hidden), F32),
        vm((all_rows, hidden), BF16), vm((all_rows, hidden), BF16),
        vm(full, BF16), vm((chunks, 3) + own[1:], BF16), vm(own, BF16),
        vm(own, BF16), vm(own, BF16),
        vm((chunks, tok, width), BF16),
        vm((2, n_dp, hidden, half), BF16), vm((2, n_dp, hidden, half), BF16),
        vm((2, n_dp, hidden, half), F32),
        dma((3, n_dp)), dma((3, n_dp)),
        dma((1,)), dma((sections,)),
        dma((chunks, experts)), dma((chunks, experts)),
        dma((chunks, GROUP)), dma((chunks, GROUP)),
        dma((chunks, experts)), dma((chunks, experts)),
        dma((chunks, GROUP)), dma((chunks, GROUP)),
        dma((chunks, 6)), dma((chunks, 6)),
        dma((chunks, experts)), dma((chunks, experts)),
        dma((chunks,)), dma((chunks,)),
        dma((2, n_dp)), dma((2, n_dp)), dma((3,)),
    ]
    flops = 14 * all_rows * hidden * width
    gate, up = pl.pallas_call(
        functools.partial(kernel, sizes),
        out_shape=(result, result),
        in_specs=[pl.BlockSpec(memory_space=pltpu.VMEM)] * 3 + [pl.BlockSpec(memory_space=pl.ANY)] * 3,
        out_specs=[pl.BlockSpec(memory_space=pltpu.VMEM)] * 2,
        scratch_shapes=scratch,
        compiler_params=pltpu.CompilerParams(
            collective_id=0, has_side_effects=True, vmem_limit_bytes=52 * 1024 * 1024),
        cost_estimate=pl.CostEstimate(
            flops=flops, bytes_accessed=12 * hidden * half, transcendentals=all_rows * hidden),
    )(saved[0, 0], cotangent, routes[0, 0], w_gate[0, 0], w_up[0, 0], w_down[0, 0])
    return gate[None, None], up[None, None]


def solution(mesh):
    weight = P(None, "pipe", "expert", "dp")
    rows = P(None, "pipe", ("expert", "dp"), None)
    in_specs = (rows, P(("expert", "dp"), "pipe"), rows, weight, weight, weight)
    return jax.shard_map(
        functools.partial(shards, mesh), mesh=mesh, in_specs=in_specs,
        out_specs=(weight, weight), check_vma=False)
```

```python
import functools

import jax
import jax.numpy as jnp
from jax import lax
from jax.experimental import pallas as pl
from jax.experimental.pallas import tpu as pltpu
from jax.sharding import PartitionSpec as P

GROUP = 4
EPSILON = 1e-06
F32 = jnp.float32
BF16 = jnp.bfloat16
MESH = pl.DeviceIdType.MESH


def dot(a, b, a_dim, b_dim):
    return lax.dot_general(a, b, (((a_dim,), (b_dim,)), ((), ())), preferred_element_type=F32)


def kernel(
    sizes,
    saved, cot, routes, wg, wu, wd,
    out_gate, out_up,
    weights, head, place, unit_send, unit_full, grad_in, grad_send, grad_full,
    gate_f, up_f, gate_grad, up_grad, part, part_recv, middle, sums, sums_recv, grad_out,
    out_send, out_recv, early,
    w_s, w_r, h_s, h_r, u1_s, u1_r, u2_s, u2_r, g1_s, g1_r, g2_s, g2_r,
    a_s, a_r, b_s, b_r, x_s, x_r, o_s, o_r,
):
    sections, experts, n_dp, chunks, rows, tok, width = sizes
    sec = lax.axis_index("pipe")
    here = lax.axis_index("expert")
    core = lax.axis_index("dp")
    e_me = here // GROUP
    q_me = here % GROUP
    last = sections - 1
    half = width // n_dp

    def copy(src, dst, s_sem, r_sem, where):
        return pltpu.make_async_remote_copy(
            src_ref=src, dst_ref=dst, send_sem=s_sem, recv_sem=r_sem,
            device_id=where, device_id_type=MESH)

    def peer(step):
        e = (e_me + step) % experts
        return e, {"expert": e * GROUP + q_me}

    q_y = q_me + 1 - 2 * (q_me % 2)
    q_z = (q_me + 2) % GROUP
    q_far = GROUP - 1 - q_me
    to_y = {"expert": e_me * GROUP + q_y}
    to_z = {"expert": e_me * GROUP + q_z}
    cut = max(128, width * 3 // 4 // 128 * 128)
    major, minor = pl.ds(0, cut), pl.ds(cut, width - cut)

    def other(step):
        c = (core + step) % n_dp
        return c, {"dp": c}

    barrier = pltpu.get_barrier_semaphore()
    friends = [peer(i)[1] for i in range(1, experts)] + [to_y, to_z]
    friends += [other(i)[1] for i in range(1, n_dp)]
    friends += [{"pipe": (sec + i) % sections} for i in range(1, sections)]
    for friend in friends:
        pl.semaphore_signal(barrier, inc=1, device_id=friend, device_id_type=MESH)
    pl.semaphore_wait(barrier, len(friends))

    def head_copy():
        return copy(cot, head.at[sec], h_s.at[0], h_r.at[sec], {"pipe": sections - 1 + 0 * sec})

    @pl.when(sec != last)
    def _():
        head_copy().start()

    def scale_of(c):
        x = saved[pl.ds(c * tok, tok), :].astype(F32)
        scale = lax.rsqrt(jnp.mean(x * x, axis=1, keepdims=True) + EPSILON)
        return x * scale, scale

    def spread_one(c, rows_b, send, full, s_sem, r_sem):
        ordered = dot(place[c], rows_b, 0, 0).astype(BF16)
        for e in range(experts):
            send[c, e] = ordered[e * rows:(e + 1) * rows]
        for i in range(1, experts):
            e, where = peer(i)
            copy(send.at[c, e], full.at[c, q_me, e_me], s_sem.at[c, e], r_sem.at[c, e_me], where).start()
        full[c, q_me, e_me] = send[c, e_me]

    def spread_two(c, send, full, s1, r1, s2, r2):
        for i in range(1, experts):
            e, where = peer(i)
            copy(send.at[c, e], full.at[c, q_me, e], s1.at[c, e], r1.at[c, e], where).wait_recv()
        group_copy(c, full, s2, r2, 0, q_me).start()
        group_copy(c, full, s2, r2, 1, q_me).start()

    def group_copy(c, full, s2, r2, kind, q):
        ref = full.at[c, q]
        if kind >= 2:
            ref = ref.at[:, :, major if kind == 2 else minor]
        return copy(ref, ref, s2.at[c, kind], r2.at[c, kind], to_z if kind % 2 else to_y)

    def relay(c, full, s2, r2):
        group_copy(c, full, s2, r2, 1, q_z).wait_recv()
        group_copy(c, full, s2, r2, 2, q_z).start()
        group_copy(c, full, s2, r2, 0, q_y).wait_recv()
        group_copy(c, full, s2, r2, 3, q_y).start()

    def spread_end(c, full, s2, r2):
        group_copy(c, full, s2, r2, 2, q_far).wait_recv()
        group_copy(c, full, s2, r2, 3, q_far).wait_recv()

    for c in range(chunks):
        chosen = routes[pl.ds(c * tok, tok), :]
        lanes = max(128, experts)
        onehot = (chosen == lax.broadcasted_iota(jnp.int32, (tok, lanes), 1)).astype(F32)
        below = (lax.broadcasted_iota(jnp.int32, (tok, tok), 1)
                 < lax.broadcasted_iota(jnp.int32, (tok, tok), 0)).astype(F32)
        ahead = dot(below.astype(BF16), onehot.astype(BF16), 1, 0)
        rank = jnp.sum(ahead * onehot, axis=1, keepdims=True)
        slot = chosen * rows + rank.astype(jnp.int32)
        place[c] = (slot == lax.broadcasted_iota(jnp.int32, (tok, tok), 1)).astype(F32).astype(BF16)
        unit, _ = scale_of(c)
        spread_one(c, unit.astype(BF16), unit_send, unit_full, u1_s, u1_r)

    for k, ref in enumerate((wg, wu, wd)):
        for i in range(1, n_dp):
            d, where = other(i)
            copy(ref, weights.at[k, core], w_s.at[k, d], w_r.at[k, core], where).start()
        weights[k, core] = ref[...]

    @pl.when(sec == last)
    def _():
        cols = width // sections
        for s in range(last):
            copy(cot, head.at[s], h_s.at[0], h_r.at[s], {"pipe": s}).wait_recv()
        for c in range(chunks):
            for s in range(sections):
                source = cot if s == last else head.at[s]
                grad_in[c, :, s * cols:(s + 1) * cols] = source[c * tok:(c + 1) * tok, :]
            spread_one(c, grad_in[c], grad_send, grad_full, g1_s, g1_r)

    for c in range(chunks):
        spread_two(c, unit_send, unit_full, u1_s, u1_r, u2_s, u2_r)

    for c in range(chunks):
        relay(c, unit_full, u2_s, u2_r)

        @pl.when(sec == last)
        def _():
            spread_two(c, grad_send, grad_full, g1_s, g1_r, g2_s, g2_r)

    for k, ref in enumerate((wg, wu, wd)):
        for i in range(1, n_dp):
            d, where = other(i)
            copy(ref, weights.at[k, d], w_s.at[k, d], w_r.at[k, d], where).wait_recv()

    per_block = GROUP if GROUP * experts * rows <= 256 else 1
    blocks = [(first, per_block) for first in range(0, GROUP, per_block)]
    block_rows = per_block * experts * rows

    def rows_of(full, c, first, count):
        return full[c, first:first + count].reshape(block_rows, width)

    def project(x, k):
        total = dot(x[:, :half], weights[k, 0], 1, 1)
        for d in range(1, n_dp):
            total = total + dot(x[:, d * half:(d + 1) * half], weights[k, d], 1, 1)
        return total

    for c in range(chunks):
        spread_end(c, unit_full, u2_s, u2_r)
        for first, count in blocks:
            x = rows_of(unit_full, c, first, count)
            at = pl.ds(c * GROUP * experts * rows + first * experts * rows, block_rows)
            gate_f[at, :] = project(x, 0)
            up_f[at, :] = project(x, 1)

    def backward(c):
        spread_end(c, grad_full, g2_s, g2_r)
        for first, count in blocks:
            at = pl.ds(c * GROUP * experts * rows + first * experts * rows, block_rows)
            hidden_grad = project(rows_of(grad_full, c, first, count), 2)
            gate = gate_f[at, :]
            up = up_f[at, :]
            sig = jax.nn.sigmoid(gate)
            gate_g = (hidden_grad * up * sig * (1.0 + gate * (1.0 - sig))).astype(BF16)
            up_g = (hidden_grad * gate * sig).astype(BF16)
            gate_grad[at, :] = gate_g
            up_grad[at, :] = up_g

            @pl.when(sec > 0)
            def _():
                for d in range(n_dp):
                    value = dot(gate_g, weights[0, d], 1, 0) + dot(up_g, weights[1, d], 1, 0)
                    part[c, first:first + count, :, :, d * half:(d + 1) * half] = (
                        value.astype(BF16).reshape(count, experts, rows, half))

        @pl.when(sec > 0)
        def _():
            for kind in (1, 3, 0, 2):
                back_copy(c, kind).start()

    def back_copy(c, kind):
        cols = major if kind in (0, 1, 4) else minor
        if kind < 4:
            q = (q_y, q_far, q_z, q_far)[kind]
            src, slot, where = part.at[c, q], kind % 2, (to_y if kind < 2 else to_z)
        else:
            src, slot, where = middle.at[c], 2, (to_z if kind == 4 else to_y)
        return copy(src.at[:, :, cols], part_recv.at[c, slot].at[:, :, cols],
                    a_s.at[c, kind], a_r.at[c, kind], where)

    def pair(c):
        for kind, cols, q in ((1, slice(0, cut), q_z), (3, slice(cut, width), q_y)):
            back_copy(c, kind).wait_recv()
            middle[c, :, :, cols] = (
                part[c, q, :, :, cols].astype(F32) + part_recv[c, 1, :, :, cols].astype(F32)
            ).astype(BF16)
            back_copy(c, 4 if kind == 1 else 5).start()

    def fold(c):
        for kind in (0, 2, 4, 5):
            back_copy(c, kind).wait_recv()
        total = part[c, q_me].astype(F32) + part_recv[c, 0].astype(F32) + part_recv[c, 2].astype(F32)
        sums[c] = total.astype(BF16)
        for i in range(1, experts):
            e, where = peer(i)
            copy(sums.at[c, e], sums_recv.at[c, e_me], b_s.at[c, e], b_r.at[c, e_me], where).start()
        sums_recv[c, e_me] = sums[c, e_me]

    def x_copy(c):
        return copy(grad_out.at[c], grad_in.at[c], x_s.at[c], x_r.at[c],
                    {"pipe": (sec + sections - 1) % sections})

    def finish(c):
        for i in range(1, experts):
            e, where = peer(i)
            copy(sums.at[c, e], sums_recv.at[c, e], b_s.at[c, e], b_r.at[c, e], where).wait_recv()
        unit_g = dot(place[c], sums_recv[c].reshape(tok, width), 1, 0)
        unit, scale = scale_of(c)
        norm = scale * (unit_g - unit * jnp.mean(unit_g * unit, axis=1, keepdims=True))
        grad_out[c] = (grad_in[c].astype(F32) + norm).astype(BF16)
        x_copy(c).start()

    chunk_rows = GROUP * experts * rows

    def outer(k, d, first, count):
        left = (gate_grad, up_grad)[k][pl.ds(first * chunk_rows, count * chunk_rows), :]
        right = unit_full[first:first + count, :, :, :, pl.ds(pl.multiple_of(d * half, 128), half)]
        return dot(left, right.reshape(count * chunk_rows, half), 0, 0)

    def sum_early():
        for k in range(2):
            for d in range(n_dp):
                early[k, d] = outer(k, d, 0, chunks // 2)

    for t in range(-3, chunks + 3):
        @pl.when(sec != last)
        def _():
            if 0 <= t + 3 < chunks:
                x_copy(t + 3).wait_recv()
                spread_one(t + 3, grad_in[t + 3], grad_send, grad_full, g1_s, g1_r)
            if 0 <= t + 2 < chunks:
                spread_two(t + 2, grad_send, grad_full, g1_s, g1_r, g2_s, g2_r)

        if 0 <= t + 1 < chunks:
            relay(t + 1, grad_full, g2_s, g2_r)
        if 0 <= t < chunks:
            if t > 0 and t == max(chunks - 2, chunks // 2):
                pl.when(sec == 0)(sum_early)
            backward(t)

        @pl.when(sec > 0)
        def _():
            if 0 <= t - 1 < chunks:
                pair(t - 1)
            if 0 <= t - 2 < chunks:
                fold(t - 2)
            if 0 <= t - 3 < chunks:
                finish(t - 3)

    if chunks > 1:
        pl.when(sec > 0)(sum_early)

    def o_copy(k, i, mine):
        d, where = other(i)
        return copy(out_send.at[k, d], out_recv.at[k, core if mine else d],
                    o_s.at[k, d], o_r.at[k, core if mine else d], where)

    def outer_all(k, d):
        value = outer(k, d, chunks // 2, chunks - chunks // 2)
        if chunks > 1:
            value = value + early[k, d]
        out_send[k, d] = value.astype(BF16)

    for k in range(2):
        for i in range(1, n_dp):
            outer_all(k, other(i)[0])
            o_copy(k, i, True).start()
    for k in range(2):
        outer_all(k, core)
    for k, out in enumerate((out_gate, out_up)):
        total = out_send[k, core].astype(F32)
        for i in range(1, n_dp):
            d, _ = other(i)
            o_copy(k, i, False).wait_recv()
            total = total + out_recv[k, d].astype(F32)
        out[...] = total.astype(BF16)

    for k, ref in enumerate((wg, wu, wd)):
        for i in range(1, n_dp):
            d, where = other(i)
            copy(ref, weights.at[k, d], w_s.at[k, d], w_r.at[k, d], where).wait_send()
    for k in range(2):
        for i in range(1, n_dp):
            o_copy(k, i, True).wait_send()

    @pl.when(sec != last)
    def _():
        head_copy().wait_send()

    for c in range(chunks):
        for i in range(1, experts):
            e, where = peer(i)
            copy(unit_send.at[c, e], unit_full.at[c, q_me, e], u1_s.at[c, e], u1_r.at[c, e], where).wait_send()
            copy(grad_send.at[c, e], grad_full.at[c, q_me, e], g1_s.at[c, e], g1_r.at[c, e], where).wait_send()
        for kind, q in enumerate((q_me, q_me, q_z, q_y)):
            group_copy(c, unit_full, u2_s, u2_r, kind, q).wait_send()
            group_copy(c, grad_full, g2_s, g2_r, kind, q).wait_send()

    @pl.when(sec > 0)
    def _():
        for c in range(chunks):
            for kind in range(6):
                back_copy(c, kind).wait_send()
            for i in range(1, experts):
                e, where = peer(i)
                copy(sums.at[c, e], sums_recv.at[c, e], b_s.at[c, e], b_r.at[c, e], where).wait_send()
            x_copy(c).wait_send()


def shards(mesh, saved, cotangent, routes, w_gate, w_up, w_down):
    sections, spots, n_dp = mesh.shape["pipe"], mesh.shape["expert"], mesh.shape["dp"]
    experts = spots // GROUP
    tokens, width = saved.shape[2], saved.shape[3]
    hidden, half = w_gate.shape[2], w_gate.shape[3]
    chunks = max(1, min(4, tokens // (experts * 16)))
    tok = tokens // chunks
    rows = tok // experts
    sizes = (sections, experts, n_dp, chunks, rows, tok, width)
    all_rows = chunks * GROUP * experts * rows
    full = (chunks, GROUP, experts, rows, width)
    own = (chunks, experts, rows, width)
    dma = pltpu.SemaphoreType.DMA
    vm = pltpu.VMEM
    result = jax.ShapeDtypeStruct((hidden, half), BF16)
    scratch = [
        vm((3, n_dp, hidden, half), BF16),
        vm((sections,) + cotangent.shape, BF16),
        vm((chunks, tok, tok), BF16),
        vm(own, BF16), vm(full, BF16),
        vm((chunks, tok, width), BF16),
        vm(own, BF16), vm(full, BF16),
        vm((all_rows, hidden), F32), vm((all_rows, hidden), F32),
        vm((all_rows, hidden), BF16), vm((all_rows, hidden), BF16),
        vm(full, BF16), vm((chunks, 3) + own[1:], BF16), vm(own, BF16),
        vm(own, BF16), vm(own, BF16),
        vm((chunks, tok, width), BF16),
        vm((2, n_dp, hidden, half), BF16), vm((2, n_dp, hidden, half), BF16),
        vm((2, n_dp, hidden, half), F32),
        dma((3, n_dp)), dma((3, n_dp)),
        dma((1,)), dma((sections,)),
        dma((chunks, experts)), dma((chunks, experts)),
        dma((chunks, GROUP)), dma((chunks, GROUP)),
        dma((chunks, experts)), dma((chunks, experts)),
        dma((chunks, GROUP)), dma((chunks, GROUP)),
        dma((chunks, 6)), dma((chunks, 6)),
        dma((chunks, experts)), dma((chunks, experts)),
        dma((chunks,)), dma((chunks,)),
        dma((2, n_dp)), dma((2, n_dp)),
    ]
    flops = 14 * all_rows * hidden * width
    gate, up = pl.pallas_call(
        functools.partial(kernel, sizes),
        out_shape=(result, result),
        in_specs=[pl.BlockSpec(memory_space=pltpu.VMEM)] * 6,
        out_specs=[pl.BlockSpec(memory_space=pltpu.VMEM)] * 2,
        scratch_shapes=scratch,
        compiler_params=pltpu.CompilerParams(
            collective_id=0, has_side_effects=True, vmem_limit_bytes=52 * 1024 * 1024),
        cost_estimate=pl.CostEstimate(
            flops=flops, bytes_accessed=12 * hidden * half, transcendentals=all_rows * hidden),
    )(saved[0, 0], cotangent, routes[0, 0], w_gate[0, 0], w_up[0, 0], w_down[0, 0])
    return gate[None, None], up[None, None]


def solution(mesh):
    weight = P(None, "pipe", "expert", "dp")
    rows = P(None, "pipe", ("expert", "dp"), None)
    in_specs = (rows, P(("expert", "dp"), "pipe"), rows, weight, weight, weight)
    return jax.shard_map(
        functools.partial(shards, mesh), mesh=mesh, in_specs=in_specs,
        out_specs=(weight, weight), check_vma=False)
```
